512 devices in a mesh: mem: 8 (over z_hi, y), lat: 4 (over x), lon: 16 (over z_lo, core).
Axes of the slice: x: 4, y: 4, z: 16 (z_hi: 2, z_lo: 8; z = z_hi * 8 + z_lo), core: 2. Of those that a mesh axis runs over, the one named last changes fastest.
Arguments:
- members: bfloat16 [128, 8, 1440, 512], P('mem', None, 'lon', 'lat'), may hold values from -6 to 6
- grad_field: float32 [8, 1440, 512], P('mem', 'lon', 'lat'), may hold values from -6 to 6
- static_std: float32 [8, 1440, 512], P(None, 'lon', 'lat'), may hold values from 0.3 to 3
- vert_mix: float32 [8, 8], replicated, may hold values from -2 to 2
- loc_weights: float32 [512, 128], P('lat'), may hold values from 0.25 to 4
Outputs:
- alpha_grad: float32 [1024, 512, 128], P(('mem', 'lon'), 'lat')
- static_grad: float32 [8, 1440, 512], P('mem', 'lon', 'lat')
The draws below stay inside these ranges and needn't reach their ends.
All inputs are finite; a program needn't handle non-finite values.
Results may differ from the reference program's by a relative error of at most 0.0057.
Values may be sent and summed in bfloat16 or wider, within the bound.
No kernel may reach another device: no remote copies, remote signals or barrier semaphores. Data moves between devices by JAX's collectives and lax.ppermute only.
A program may use at most 64 MiB of HBM per device.

```python
import math
import jax
import jax.numpy as jnp
from jax import lax

LEV = 8
NLON = 1440
NLAT = 512
KLON = 512
KLAT = 128
MEM = 128


def block_scale(key, extent, cuts, least, largest):
    loudness = 1.0
    for position, blocks in cuts:
        draws = jax.random.uniform(jax.random.fold_in(jax.random.fold_in(key, 6), position), (blocks,), jnp.float32, least / len(cuts), largest / len(cuts))
        loudness = loudness * jnp.repeat(jnp.exp(draws), extent[position] // blocks).reshape((-1,) + (1,) * (len(extent) - 1 - position))
    return loudness


def noise(own_key, dims, scale, limit, cuts=(), kind=jnp.bfloat16):
    values = scale * jax.random.normal(own_key, dims, jnp.float32)
    if cuts:
        values = values * block_scale(own_key, dims, cuts, -0.22, 0.18)
    return jnp.clip(values, -limit, limit).astype(kind)


def setup_inputs(seed: int = 0) -> dict:
    splits = jax.random.split(jax.random.key(seed), 6)
    members = noise(splits[0], (MEM, LEV, NLON, NLAT), 1.0, 6.0, ((0, 8), (2, 16), (3, 4)))
    grad_field = noise(splits[1], (LEV, NLON, NLAT), 1.0, 6.0, ((0, 8), (1, 16), (2, 4)), jnp.float32)
    static_std = jnp.clip(jnp.exp(math.log(3.0) - 2.3025851 * jax.random.uniform(splits[2], (LEV, NLON, NLAT), jnp.float32) ** block_scale(splits[2], (LEV, NLON, NLAT), ((1, 16), (2, 4)), -0.2, 0.2)), 0.3, 3.0)
    vert_mix = noise(splits[3], (LEV, LEV), LEV ** -0.5, 2.0, (), jnp.float32)
    loc_weights = jnp.clip(jnp.exp(math.log(4.0) - 2.7725887 * jax.random.uniform(splits[4], (KLON, KLAT), jnp.float32) ** block_scale(splits[4], (KLON, KLAT), ((0, 4),), -0.2, 0.2)), 0.25, 4.0)
    return dict(members=members, grad_field=grad_field, static_std=static_std, vert_mix=vert_mix, loc_weights=loc_weights)


def lon_table_make(n_lon, k_lon):
    cells = jnp.arange(n_lon, dtype=jnp.int32)[:, None]
    waves = jnp.arange(k_lon // 2, dtype=jnp.int32)[None, :]
    cos_phase = (cells * waves % n_lon).astype(jnp.float32)
    sin_phase = (cells * (waves + 1) % n_lon).astype(jnp.float32)
    factor = jnp.sqrt(jnp.float32(2.0) / n_lon)
    angle_cos = jnp.float32(2.0 * jnp.pi) * cos_phase / n_lon
    angle_sin = jnp.float32(2.0 * jnp.pi) * sin_phase / n_lon
    table = jnp.concatenate([jnp.cos(angle_cos), jnp.sin(angle_sin)], axis=1) * factor
    return table.astype(jnp.bfloat16)

def lat_table_make(first, count, n_lat, k_lat):
    cells = first + jnp.arange(count, dtype=jnp.int32)[:, None]
    waves = jnp.arange(k_lat, dtype=jnp.int32)[None, :]
    phase = ((2 * cells + 1) * waves % (4 * n_lat)).astype(jnp.float32)
    angle = jnp.float32(jnp.pi) * phase / (2 * n_lat)
    return (jnp.cos(angle) * jnp.sqrt(jnp.float32(2.0) / n_lat)).astype(jnp.bfloat16)

def reference(members, grad_field, static_std, vert_mix, loc_weights):
    lon_table = lon_table_make(NLON, KLON).astype(jnp.float32)
    lat_table = lat_table_make(jnp.int32(0), NLAT, NLAT, KLAT).astype(jnp.float32)

    def one_member(member):
        product = (member.astype(jnp.float32) * grad_field).astype(jnp.bfloat16)
        zonal = jnp.einsum('lnc,nk->lkc', product.astype(jnp.float32), lon_table).astype(jnp.bfloat16)
        summed = jnp.einsum('lkc,cq->lkq', zonal.astype(jnp.float32), lat_table)
        return summed * loc_weights[None]
    alpha_grad = lax.map(one_member, members).reshape(MEM * LEV, KLON, KLAT)
    static_grad = jnp.einsum('lj,lxy->jxy', vert_mix, static_std * grad_field, precision=lax.Precision.HIGHEST)
    return (alpha_grad, static_grad)
```

```python
import jax
import jax.numpy as jnp
from jax import lax
from jax.experimental import pallas as pl
from jax.experimental.pallas import tpu as pltpu
from jax.sharding import PartitionSpec as P

NLON = 1440
NLAT = 512
KLON = 512
KLAT = 128
PAIR = 2
TILE = 8


def cosine(phase, period):
    return jnp.cos(jnp.float32(2.0 * jnp.pi) * (phase % period).astype(jnp.float32) / period)


def lon_table_make(n_lon, k_lon, blocks, rows, waves):
    band = n_lon // blocks
    column = waves
    level = column // (k_lon // 4) % PAIR
    number = column // (k_lon // 4 * PAIR) * (k_lon // 4) + column % (k_lon // 4)
    sine = number >= k_lon // 2
    wave = jnp.where(sine, number - k_lon // 2 + 1, number)[None, :]
    shift = jnp.where(sine, n_lon // 4, 0)[None, :]
    row = jnp.arange(rows, dtype=jnp.int32)[:, None]
    starts = jnp.arange(blocks, dtype=jnp.int32)[:, None] * band * wave - shift
    places = row % band * wave
    factor = jnp.sqrt(jnp.float32(2.0) / n_lon)
    cos_start, sin_start = cosine(starts, n_lon) * factor, cosine(starts - n_lon // 4, n_lon) * factor
    own = row // band == level[None, :]
    cos_place = jnp.where(own, cosine(places, n_lon), 0.0)
    sin_place = jnp.where(own, cosine(places - n_lon // 4, n_lon), 0.0)
    table = cos_start[:, None] * cos_place[None] - sin_start[:, None] * sin_place[None]
    return table.astype(jnp.bfloat16).reshape(blocks * rows, PAIR * k_lon)


def lat_table_make(cells, n_lat, k_lat):
    waves = jnp.arange(k_lat, dtype=jnp.int32)[None, :]
    phase = ((2 * cells[:, None] + 1) * waves % (4 * n_lat)).astype(jnp.float32)
    angle = jnp.float32(jnp.pi) * phase / (2 * n_lat)
    return (jnp.cos(angle) * jnp.sqrt(jnp.float32(2.0) / n_lat)).astype(jnp.bfloat16)


def after(value, earlier):
    return lax.optimization_barrier((value, earlier))[0]


def ring(size, step, groups=1):
    return [(g * size + i, g * size + (i + step) % size) for g in range(groups) for i in range(size)]


def from_ahead(field, axis, groups):
    return [lax.ppermute(field, axis, ring(4, -step, groups)) for step in (1, 2, 3)]


def by_position(mine, ahead, me):
    turned = jnp.stack([mine, *ahead, mine, *ahead[:2]])
    return lax.dynamic_slice_in_dim(turned, (4 - me) % 4, 4, 0)


def spread_kernel(members_ref, out_ref, wide, both):
    count, lon, levels, _ = members_ref.shape
    both[...] = jnp.zeros_like(both)
    for m in range(count):
        wide[m % 2, : lon * levels] = members_ref[m].astype(jnp.float32).reshape(lon * levels, -1)
        for part in range(levels // PAIR):
            for place in range(PAIR):
                both[part, place * lon : (place + 1) * lon] = wide[
                    m % 2, pl.ds(part * PAIR + place, lon, stride=levels), :
                ]
            out_ref[part, m] = both[part].astype(jnp.bfloat16)


def spread(members, rows):
    count, lon, levels, lat = members.shape
    step = min(2, count)
    return pl.pallas_call(
        spread_kernel,
        out_shape=jax.ShapeDtypeStruct((levels // PAIR, count, rows, lat), members.dtype),
        grid=(count // step,),
        in_specs=[pl.BlockSpec((step, lon, levels, lat), lambda i: (i, 0, 0, 0))],
        out_specs=pl.BlockSpec((levels // PAIR, step, rows, lat), lambda i: (0, i, 0, 0)),
        scratch_shapes=[
            pltpu.VMEM((2, (lon + TILE) * levels, lat), jnp.float32),
            pltpu.VMEM((levels // PAIR, rows, lat), jnp.float32),
        ],
        compiler_params=pltpu.CompilerParams(vmem_limit_bytes=56 * 2**20),
        cost_estimate=pl.CostEstimate(flops=members.size, bytes_accessed=4 * members.size, transcendentals=0),
    )(members)


def lat_sums_kernel(x_ref, parts_ref, grads_ref, table_ref, out_ref):
    x = x_ref[0]
    for m in range(out_ref.shape[0]):
        product = [
            (parts_ref[part, m].astype(jnp.float32) * grads_ref[(part + 4 - x) % 4]).astype(jnp.bfloat16)
            for part in range(4)
        ]
        sums = jnp.dot(
            jnp.concatenate(product, axis=1), table_ref[...], preferred_element_type=jnp.float32
        )
        out_ref[m] = sums.astype(jnp.bfloat16)


def lat_sums(x, parts, grads, table):
    bands, count, rows, lat = parts.shape
    waves = table.shape[1]
    step = min(4, count)
    return pl.pallas_call(
        lat_sums_kernel,
        out_shape=jax.ShapeDtypeStruct((count, rows, waves), jnp.bfloat16),
        grid=(count // step,),
        in_specs=[
            pl.BlockSpec(memory_space=pltpu.SMEM),
            pl.BlockSpec((bands, step, rows, lat), lambda i: (0, i, 0, 0)),
            pl.BlockSpec((bands, rows, lat), lambda i: (0, 0, 0)),
            pl.BlockSpec((bands * lat, waves), lambda i: (0, 0)),
        ],
        out_specs=pl.BlockSpec((step, rows, waves), lambda i: (i, 0, 0)),
        compiler_params=pltpu.CompilerParams(vmem_limit_bytes=24 * 2**20),
        cost_estimate=pl.CostEstimate(
            flops=2 * parts.size * waves, bytes_accessed=2 * parts.size, transcendentals=0
        ),
    )(jnp.reshape(x, (1,)).astype(jnp.int32), parts, grads, table)


def local(members, grad_field, static_std, vert_mix, loc_weights):
    mem_local, levels, lon_local, lat_local = members.shape
    mem = lax.axis_index("mem")
    half_z, y = mem // 4, mem % 4
    x = lax.axis_index("lat")
    rows = -(-PAIR * lon_local // TILE) * TILE

    sent = spread(members.transpose(0, 2, 1, 3), rows)
    parts = lax.all_to_all(sent, "lat", split_axis=0, concat_axis=0, tiled=True)

    lat_table = lat_table_make(after(jnp.arange(NLAT, dtype=jnp.int32), sent), NLAT, KLAT)
    own_grad = after(grad_field[0], lat_table)
    far_grad = lax.ppermute(own_grad, "mem", [(i, (i + 4) % 8) for i in range(8)])
    low = jnp.where(half_z == 0, own_grad, far_grad)
    high = jnp.where(half_z == 0, far_grad, own_grad)
    halves = jnp.stack([low, high])
    grads = by_position(halves, from_ahead(halves, "mem", 2), y)
    grads = grads.transpose(1, 0, 2, 3).reshape(levels, lon_local, lat_local)
    pairs = grads.reshape(4, PAIR * lon_local, lat_local)
    pairs = jnp.pad(pairs, ((0, 0), (0, rows - PAIR * lon_local), (0, 0)))

    def pair(step):
        return lax.dynamic_index_in_dim(pairs, (x + step) % 4, 0, keepdims=False)

    met = jnp.stack(
        [pair(0)] + [lax.ppermute(pair(4 - step), "lat", ring(4, -step)) for step in (1, 2, 3)]
    )

    sums = lat_sums(x, parts, met, lat_table)

    whole = lax.all_to_all(sums, "lon", split_axis=0, concat_axis=0, tiled=True)
    columns = after(jnp.arange(PAIR * KLON, dtype=jnp.int32), sums)
    lon_table = lon_table_make(NLON, KLON, mem_local, rows, columns)
    zonal = jnp.einsum(
        "nk,nq->kq", lon_table, whole.reshape(mem_local * rows, KLAT), preferred_element_type=jnp.float32
    ).astype(jnp.bfloat16)
    zonal = zonal.reshape(4, PAIR, KLON // 4, KLAT)
    alpha = lax.all_to_all(zonal, "lat", split_axis=0, concat_axis=0, tiled=True)
    alpha_grad = alpha.reshape(levels, KLON // 4, KLAT).astype(jnp.float32) * loc_weights[None]

    mix = after(lax.dynamic_index_in_dim(vert_mix, mem, 1, keepdims=False), sums)
    static_grad = jnp.sum(mix[:, None, None] * (static_std * grads), axis=0)
    return (alpha_grad, static_grad[None])


def solution(mesh):
    in_specs = (
        P("mem", None, "lon", "lat"),
        P("mem", "lon", "lat"),
        P(None, "lon", "lat"),
        P(),
        P("lat", None),
    )
    out_specs = (P(("mem", "lon"), "lat", None), P("mem", "lon", "lat"))
    return jax.shard_map(local, mesh=mesh, in_specs=in_specs, out_specs=out_specs, check_vma=False)
```

```python
import jax
import jax.numpy as jnp
from jax import lax
from jax.experimental import pallas as pl
from jax.experimental.pallas import tpu as pltpu
from jax.sharding import PartitionSpec as P

NLON = 1440
NLAT = 512
KLON = 512
KLAT = 128
PAIR = 2
TILE = 8


def cosine(phase, period):
    return jnp.cos(jnp.float32(2.0 * jnp.pi) * (phase % period).astype(jnp.float32) / period)


def lon_table_make(n_lon, k_lon, blocks, rows, waves):
    band = n_lon // blocks
    whole = band // TILE * TILE
    column = waves
    level = column // (k_lon // 4) % PAIR
    number = column // (k_lon // 4 * PAIR) * (k_lon // 4) + column % (k_lon // 4)
    sine = number >= k_lon // 2
    wave = jnp.where(sine, number - k_lon // 2 + 1, number)[None, :]
    shift = jnp.where(sine, n_lon // 4, 0)[None, :]
    row = jnp.arange(rows, dtype=jnp.int32)[:, None]
    starts = jnp.arange(blocks, dtype=jnp.int32)[:, None] * band * wave - shift
    last = row - PAIR * whole
    place = jnp.where(last < 0, row % whole, whole + last % (band - whole))
    row_level = jnp.where(last < 0, row // whole, last // (band - whole))
    places = place * wave
    factor = jnp.sqrt(jnp.float32(2.0) / n_lon)
    cos_start, sin_start = cosine(starts, n_lon) * factor, cosine(starts - n_lon // 4, n_lon) * factor
    own = row_level == level[None, :]
    cos_place = jnp.where(own, cosine(places, n_lon), 0.0)
    sin_place = jnp.where(own, cosine(places - n_lon // 4, n_lon), 0.0)
    table = cos_start[:, None] * cos_place[None] - sin_start[:, None] * sin_place[None]
    return table.astype(jnp.bfloat16).reshape(blocks * rows, PAIR * k_lon)


def lat_table_make(cells, n_lat, k_lat):
    waves = jnp.arange(k_lat, dtype=jnp.int32)[None, :]
    phase = ((2 * cells[:, None] + 1) * waves % (4 * n_lat)).astype(jnp.float32)
    angle = jnp.float32(jnp.pi) * phase / (2 * n_lat)
    return (jnp.cos(angle) * jnp.sqrt(jnp.float32(2.0) / n_lat)).astype(jnp.bfloat16)


def after(value, earlier):
    return lax.optimization_barrier((value, earlier))[0]


def partners(size, flip):
    return [(i, i ^ flip) for i in range(size)]


def from_ahead(field):
    rings = [[(i, i // 4 * 4 + (i - step) % 4) for i in range(8)] for step in (1, 2, 3)]
    return [lax.ppermute(field, "mem", pairs) for pairs in rings]


def by_position(mine, ahead, me):
    turned = jnp.stack([mine, *ahead, mine, *ahead[:2]])
    return lax.dynamic_slice_in_dim(turned, (4 - me) % 4, 4, 0)


def pack_rows(fields, rows):
    lon = fields[0].shape[0]
    whole = lon // TILE * TILE
    empty = jnp.zeros((rows - len(fields) * lon, fields[0].shape[1]), fields[0].dtype)
    return jnp.concatenate([*[f[:whole] for f in fields], *[f[whole:] for f in fields], empty])


def spread_kernel(members_ref, out_ref, wide):
    count, lon, levels, lat = members_ref.shape
    whole = lon // TILE * TILE
    rows = out_ref.shape[2]
    for m in range(count):
        wide[m % 2] = members_ref[m].astype(jnp.float32).reshape(lon * levels, lat)
        for part in range(levels // PAIR):
            firsts = [part * PAIR + place for place in range(PAIR)]
            pieces = [wide[m % 2, pl.ds(first, whole, stride=levels), :] for first in firsts]
            lasts = [
                wide[m % 2, pl.ds(first + n * levels, 1), :] for first in firsts for n in range(whole, lon)
            ]
            empty = jnp.zeros((rows - PAIR * lon, lat), jnp.float32)
            out_ref[part, m] = jnp.concatenate([*pieces, *lasts, empty]).astype(jnp.bfloat16)


def spread(members, rows):
    count, lon, levels, lat = members.shape
    step = min(4, count)
    return pl.pallas_call(
        spread_kernel,
        out_shape=jax.ShapeDtypeStruct((levels // PAIR, count, rows, lat), members.dtype),
        grid=(count // step,),
        in_specs=[pl.BlockSpec((step, lon, levels, lat), lambda i: (i, 0, 0, 0))],
        out_specs=pl.BlockSpec((levels // PAIR, step, rows, lat), lambda i: (0, i, 0, 0)),
        scratch_shapes=[pltpu.VMEM((2, lon * levels, lat), jnp.float32)],
        compiler_params=pltpu.CompilerParams(vmem_limit_bytes=56 * 2**20),
        cost_estimate=pl.CostEstimate(flops=members.size, bytes_accessed=4 * members.size, transcendentals=0),
    )(members)


def lat_sums_kernel(parts_ref, grads_ref, table_ref, out_ref, packed):
    bands, count, rows, _ = parts_ref.shape

    @pl.when(pl.program_id(0) == 0)
    def _():
        for part in range(bands):
            packed[part] = pack_rows([grads_ref[part, place] for place in range(PAIR)], rows)

    for m in range(count):
        product = [
            (parts_ref[part, m].astype(jnp.float32) * packed[part]).astype(jnp.bfloat16)
            for part in range(bands)
        ]
        sums = jnp.dot(
            jnp.concatenate(product, axis=1), table_ref[...], preferred_element_type=jnp.float32
        )
        out_ref[m] = sums.astype(jnp.bfloat16)


def lat_sums(parts, grads, table):
    bands, count, rows, lat = parts.shape
    waves = table.shape[1]
    step = min(4, count)
    return pl.pallas_call(
        lat_sums_kernel,
        out_shape=pltpu.HBM((count, rows, waves), jnp.bfloat16),
        grid=(count // step,),
        in_specs=[
            pl.BlockSpec((bands, step, rows, lat), lambda i: (0, i, 0, 0)),
            pl.BlockSpec(grads.shape, lambda i: (0, 0, 0, 0)),
            pl.BlockSpec((bands * lat, waves), lambda i: (0, 0)),
        ],
        out_specs=pl.BlockSpec((step, rows, waves), lambda i: (i, 0, 0)),
        scratch_shapes=[pltpu.VMEM((bands, rows, lat), jnp.float32)],
        compiler_params=pltpu.CompilerParams(vmem_limit_bytes=24 * 2**20),
        cost_estimate=pl.CostEstimate(
            flops=2 * parts.size * waves, bytes_accessed=2 * parts.size, transcendentals=0
        ),
    )(parts, grads, table)


def local(members, grad_field, static_std, vert_mix, loc_weights):
    mem_local, levels, lon_local, lat_local = members.shape
    mem = lax.axis_index("mem")
    half_z, y = mem // 4, mem % 4
    rows = -(-PAIR * lon_local // TILE) * TILE

    sent = spread(members.transpose(0, 2, 1, 3), rows)
    parts = lax.all_to_all(sent, "lat", split_axis=0, concat_axis=0, tiled=True)

    lat_table = lat_table_make(after(jnp.arange(NLAT, dtype=jnp.int32), sent), NLAT, KLAT)
    own_grad = after(grad_field, lat_table)[0]
    far_grad = lax.ppermute(own_grad, "mem", partners(8, 4))
    mine = jnp.stack([jnp.where(half_z == 0, own_grad, far_grad), jnp.where(half_z == 0, far_grad, own_grad)])
    grads = by_position(mine, from_ahead(mine), y)
    grads = grads.transpose(1, 0, 2, 3).reshape(levels, lon_local, lat_local)
    pairs = after(grads.reshape(4, PAIR, lon_local, lat_local), parts)
    met = lax.all_to_all(pairs, "lat", split_axis=0, concat_axis=0, tiled=True)
    sums = lat_sums(parts, met, lat_table)

    whole = lax.all_to_all(sums, "lon", split_axis=0, concat_axis=0, tiled=True)
    columns = after(jnp.arange(PAIR * KLON, dtype=jnp.int32), sums)
    lon_table = lon_table_make(NLON, KLON, mem_local, rows, columns)
    zonal = jnp.einsum(
        "nk,nq->kq", lon_table, whole.reshape(mem_local * rows, KLAT), preferred_element_type=jnp.float32
    ).astype(jnp.bfloat16)
    zonal = zonal.reshape(4, PAIR, KLON // 4, KLAT)
    alpha = lax.all_to_all(zonal, "lat", split_axis=0, concat_axis=0, tiled=True)
    alpha_grad = alpha.reshape(levels, KLON // 4, KLAT).astype(jnp.float32) * loc_weights[None]

    mix = after(lax.dynamic_index_in_dim(vert_mix, mem, 1, keepdims=False), sums)
    static_grad = jnp.sum(mix[:, None, None] * (static_std * grads), axis=0)
    return (alpha_grad, static_grad[None])


def solution(mesh):
    in_specs = (
        P("mem", None, "lon", "lat"),
        P("mem", "lon", "lat"),
        P(None, "lon", "lat"),
        P(),
        P("lat", None),
    )
    out_specs = (P(("mem", "lon"), "lat", None), P("mem", "lon", "lat"))
    return jax.shard_map(local, mesh=mesh, in_specs=in_specs, out_specs=out_specs, check_vma=False)
```

```python
import jax
import jax.numpy as jnp
from jax import lax
from jax.experimental import pallas as pl
from jax.experimental.pallas import tpu as pltpu
from jax.sharding import PartitionSpec as P

NLON = 1440
NLAT = 512
KLON = 512
KLAT = 128
PAIR = 2
TILE = 8


def cosine(phase, period):
    return jnp.cos(jnp.float32(2.0 * jnp.pi) * (phase % period).astype(jnp.float32) / period)


def lon_table_make(n_lon, places, waves):
    half = waves.shape[0] // 2
    sine = waves >= half
    number = jnp.where(sine, waves - half + 1, waves)[:, None]
    phase = number * places[None, :] - jnp.where(sine, n_lon // 4, 0)[:, None]
    return cosine(phase, n_lon) * jnp.sqrt(jnp.float32(2.0) / n_lon)


def lon_tables_make(n_lon, blocks, waves):
    band = n_lon // blocks
    whole = band // TILE * TILE
    left = band - whole
    column = jnp.arange(blocks * whole, dtype=jnp.int32)
    main = lon_table_make(n_lon, column // whole * band + column % whole, waves)
    column = jnp.arange(blocks * TILE, dtype=jnp.int32)
    row = column % TILE
    tail = lon_table_make(n_lon, column // TILE * band + whole + row % left, waves)
    tails = [jnp.where((row // left == level)[None, :], tail, 0.0) for level in range(PAIR)]
    return main.astype(jnp.bfloat16), jnp.stack(tails).astype(jnp.bfloat16)


def lat_table_make(cells, n_lat, k_lat):
    waves = jnp.arange(k_lat, dtype=jnp.int32)[None, :]
    phase = ((2 * cells[:, None] + 1) * waves % (4 * n_lat)).astype(jnp.float32)
    angle = jnp.float32(jnp.pi) * phase / (2 * n_lat)
    return (jnp.cos(angle) * jnp.sqrt(jnp.float32(2.0) / n_lat)).astype(jnp.bfloat16)


def after(value, earlier):
    return lax.optimization_barrier((value, earlier))[0]


def partners(size, flip):
    return [(i, i ^ flip) for i in range(size)]


def pack_rows(fields, rows):
    lon = fields[0].shape[0]
    whole = lon // TILE * TILE
    empty = jnp.zeros((rows - len(fields) * lon, fields[0].shape[1]), fields[0].dtype)
    return jnp.concatenate([*[f[:whole] for f in fields], *[f[whole:] for f in fields], empty])


def spread_kernel(members_ref, out_ref, wide):
    count, lon, levels, lat = members_ref.shape
    whole = lon // TILE * TILE
    rows = out_ref.shape[2]
    for m in range(count):
        wide[m % 2] = members_ref[m].astype(jnp.float32).reshape(lon * levels, lat)
        for part in range(levels // PAIR):
            firsts = [part * PAIR + place for place in range(PAIR)]
            pieces = [wide[m % 2, pl.ds(first, whole, stride=levels), :] for first in firsts]
            lasts = [
                wide[m % 2, pl.ds(first + n * levels, 1), :] for first in firsts for n in range(whole, lon)
            ]
            empty = jnp.zeros((rows - PAIR * lon, lat), jnp.float32)
            out_ref[part, m] = jnp.concatenate([*pieces, *lasts, empty]).astype(jnp.bfloat16)


def spread(members, rows):
    count, lon, levels, lat = members.shape
    step = min(4, count)
    return pl.pallas_call(
        spread_kernel,
        out_shape=jax.ShapeDtypeStruct((levels // PAIR, count, rows, lat), members.dtype),
        grid=(count // step,),
        in_specs=[pl.BlockSpec((step, lon, levels, lat), lambda i: (i, 0, 0, 0))],
        out_specs=pl.BlockSpec((levels // PAIR, step, rows, lat), lambda i: (0, i, 0, 0)),
        scratch_shapes=[pltpu.VMEM((2, lon * levels, lat), jnp.float32)],
        compiler_params=pltpu.CompilerParams(vmem_limit_bytes=56 * 2**20),
        cost_estimate=pl.CostEstimate(flops=members.size, bytes_accessed=4 * members.size, transcendentals=0),
    )(members)


def lat_sums_kernel(x_ref, parts_ref, grads_ref, table_ref, out_ref, packed):
    bands, count, rows, _ = parts_ref.shape
    x = x_ref[0]

    @pl.when(pl.program_id(0) == 0)
    def _():
        for part in range(bands):
            packed[part] = pack_rows([grads_ref[(part + 4 - x) % 4, place] for place in range(PAIR)], rows)

    for m in range(count):
        product = [
            (parts_ref[part, m].astype(jnp.float32) * packed[part]).astype(jnp.bfloat16)
            for part in range(bands)
        ]
        sums = jnp.dot(
            jnp.concatenate(product, axis=1), table_ref[...], preferred_element_type=jnp.float32
        )
        out_ref[m] = sums.astype(jnp.bfloat16)


def lat_sums(x, parts, grads, table):
    bands, count, rows, lat = parts.shape
    waves = table.shape[1]
    step = min(4, count)
    return pl.pallas_call(
        lat_sums_kernel,
        out_shape=pltpu.HBM((count, rows, waves), jnp.bfloat16),
        grid=(count // step,),
        in_specs=[
            pl.BlockSpec(memory_space=pltpu.SMEM),
            pl.BlockSpec((bands, step, rows, lat), lambda i: (0, i, 0, 0)),
            pl.BlockSpec(grads.shape, lambda i: (0, 0, 0, 0)),
            pl.BlockSpec((bands * lat, waves), lambda i: (0, 0)),
        ],
        out_specs=pl.BlockSpec((step, rows, waves), lambda i: (i, 0, 0)),
        scratch_shapes=[pltpu.VMEM((bands, rows, lat), jnp.float32)],
        compiler_params=pltpu.CompilerParams(vmem_limit_bytes=24 * 2**20),
        cost_estimate=pl.CostEstimate(
            flops=2 * parts.size * waves, bytes_accessed=2 * parts.size, transcendentals=0
        ),
    )(jnp.reshape(x, (1,)).astype(jnp.int32), parts, grads, table)


def zonal_kernel(rows_ref, main_ref, tails_ref, out_ref):
    blocks = rows_ref.shape[0]
    whole = main_ref.shape[1] // blocks
    bands = [rows_ref[block].astype(jnp.float32) for block in range(blocks)]
    last = jnp.concatenate([band[PAIR * whole :] for band in bands]).astype(jnp.bfloat16)
    for level in range(PAIR):
        first = [band[level * whole : (level + 1) * whole] for band in bands]
        sums = jnp.dot(
            main_ref[...], jnp.concatenate(first).astype(jnp.bfloat16), preferred_element_type=jnp.float32
        ) + jnp.dot(tails_ref[level], last, preferred_element_type=jnp.float32)
        quarter = sums.shape[0] // 4
        for part in range(4):
            out_ref[part, level] = sums[part * quarter : (part + 1) * quarter].astype(jnp.bfloat16)


def zonal_sums(rows, main, tails):
    waves, k_lat = main.shape[0], rows.shape[2]
    return pl.pallas_call(
        zonal_kernel,
        out_shape=pltpu.HBM((4, PAIR, waves // 4, k_lat), jnp.bfloat16),
        in_specs=[pl.BlockSpec(memory_space=pltpu.VMEM)] * 3,
        out_specs=pl.BlockSpec(memory_space=pltpu.VMEM),
        compiler_params=pltpu.CompilerParams(vmem_limit_bytes=24 * 2**20),
        cost_estimate=pl.CostEstimate(
            flops=2 * PAIR * main.size * k_lat, bytes_accessed=2 * (main.size + rows.size), transcendentals=0
        ),
    )(rows, main, tails)


def local(members, grad_field, static_std, vert_mix, loc_weights):
    mem_local, levels, lon_local, lat_local = members.shape
    mem = lax.axis_index("mem")
    half_z, y = mem // 4, mem % 4
    x = lax.axis_index("lat")
    rows = -(-PAIR * lon_local // TILE) * TILE

    sent = spread(members.transpose(0, 2, 1, 3), rows)
    parts = lax.all_to_all(sent, "lat", split_axis=0, concat_axis=0, tiled=True)

    lat_table = lat_table_make(after(jnp.arange(NLAT, dtype=jnp.int32), sent), NLAT, KLAT)
    own_grad = grad_field[0]
    far_grad = lax.ppermute(own_grad, "mem", partners(8, 4))
    mine = jnp.stack([jnp.where(half_z == 0, own_grad, far_grad), jnp.where(half_z == 0, far_grad, own_grad)])
    beside = lax.ppermute(mine, "mem", partners(8, 1))
    two = jnp.stack([jnp.where(y % 2 == 0, mine, beside), jnp.where(y % 2 == 0, beside, mine)])
    others = lax.ppermute(two, "mem", partners(8, 3))
    grads = jnp.concatenate([jnp.where(y < 2, two, others), jnp.where(y < 2, others, two)])
    grads = grads.transpose(1, 0, 2, 3).reshape(levels, lon_local, lat_local)
    pairs = grads.reshape(4, PAIR, lon_local, lat_local)

    def pair(step):
        return lax.dynamic_index_in_dim(pairs, (x + step) % 4, 0, keepdims=False)

    met = jnp.stack(
        [pair(0)]
        + [lax.ppermute(pair(4 - d), "lat", [(i, (i - d) % 4) for i in range(4)]) for d in (1, 2, 3)]
    )
    sums = lat_sums(x, parts, met, lat_table)

    whole = lax.all_to_all(sums, "lon", split_axis=0, concat_axis=0, tiled=True)
    waves = after(jnp.arange(KLON, dtype=jnp.int32), sums)
    zonal = zonal_sums(whole, *lon_tables_make(NLON, mem_local, waves))
    alpha = lax.all_to_all(zonal, "lat", split_axis=0, concat_axis=0, tiled=True)
    alpha_grad = alpha.reshape(levels, KLON // 4, KLAT).astype(jnp.float32) * loc_weights[None]

    mix = after(lax.dynamic_index_in_dim(vert_mix, mem, 1, keepdims=False), sums)
    static_grad = jnp.sum(mix[:, None, None] * (static_std * grads), axis=0)
    return (alpha_grad, static_grad[None])


def solution(mesh):
    in_specs = (
        P("mem", None, "lon", "lat"),
        P("mem", "lon", "lat"),
        P(None, "lon", "lat"),
        P(),
        P("lat", None),
    )
    out_specs = (P(("mem", "lon"), "lat", None), P("mem", "lon", "lat"))
    return jax.shard_map(local, mesh=mesh, in_specs=in_specs, out_specs=out_specs, check_vma=False)
```

```python
import jax
import jax.numpy as jnp
from jax import lax
from jax.experimental import pallas as pl
from jax.experimental.pallas import tpu as pltpu
from jax.sharding import PartitionSpec as P

NLON = 1440
NLAT = 512
KLON = 512
KLAT = 128
PAIR = 2
TILE = 8


def cosine(phase, period):
    return jnp.cos(jnp.float32(2.0 * jnp.pi) * (phase % period).astype(jnp.float32) / period)


def lon_table_make(n_lon, places, waves):
    half = waves.shape[0] // 2
    sine = waves >= half
    number = jnp.where(sine, waves - half + 1, waves)[:, None]
    phase = number * places[None, :] - jnp.where(sine, n_lon // 4, 0)[:, None]
    return cosine(phase, n_lon) * jnp.sqrt(jnp.float32(2.0) / n_lon)


def lon_tables_make(n_lon, blocks, waves):
    band = n_lon // blocks
    whole = band // TILE * TILE
    left = band - whole
    column = jnp.arange(blocks * whole, dtype=jnp.int32)
    main = lon_table_make(n_lon, column // whole * band + column % whole, waves)
    column = jnp.arange(blocks * TILE, dtype=jnp.int32)
    row = column % TILE
    tail = lon_table_make(n_lon, column // TILE * band + whole + row % left, waves)
    tails = [jnp.where((row // left == level)[None, :], tail, 0.0) for level in range(PAIR)]
    return main.astype(jnp.bfloat16), jnp.stack(tails).astype(jnp.bfloat16)


def lat_table_make(cells, n_lat, k_lat):
    waves = jnp.arange(k_lat, dtype=jnp.int32)[None, :]
    phase = ((2 * cells[:, None] + 1) * waves % (4 * n_lat)).astype(jnp.float32)
    angle = jnp.float32(jnp.pi) * phase / (2 * n_lat)
    return (jnp.cos(angle) * jnp.sqrt(jnp.float32(2.0) / n_lat)).astype(jnp.bfloat16)


def after(value, earlier):
    return lax.optimization_barrier((value, earlier))[0]


def partners(size, flip):
    return [(i, i ^ flip) for i in range(size)]


def pack_rows(fields, rows):
    lon = fields[0].shape[0]
    whole = lon // TILE * TILE
    empty = jnp.zeros((rows - len(fields) * lon, fields[0].shape[1]), fields[0].dtype)
    return jnp.concatenate([*[f[:whole] for f in fields], *[f[whole:] for f in fields], empty])


def spread_kernel(members_ref, out_ref, wide):
    count, lon, levels, lat = members_ref.shape
    whole = lon // TILE * TILE
    rows = out_ref.shape[2]
    for m in range(count):
        wide[m % 2] = members_ref[m].astype(jnp.float32).reshape(lon * levels, lat)
        for part in range(levels // PAIR):
            firsts = [part * PAIR + place for place in range(PAIR)]
            pieces = [wide[m % 2, pl.ds(first, whole, stride=levels), :] for first in firsts]
            lasts = [
                wide[m % 2, pl.ds(first + n * levels, 1), :] for first in firsts for n in range(whole, lon)
            ]
            empty = jnp.zeros((rows - PAIR * lon, lat), jnp.float32)
            out_ref[part, m] = jnp.concatenate([*pieces, *lasts, empty]).astype(jnp.bfloat16)


def spread(members, rows):
    count, lon, levels, lat = members.shape
    step = min(4, count)
    return pl.pallas_call(
        spread_kernel,
        out_shape=jax.ShapeDtypeStruct((levels // PAIR, count, rows, lat), members.dtype),
        grid=(count // step,),
        in_specs=[pl.BlockSpec((step, lon, levels, lat), lambda i: (i, 0, 0, 0))],
        out_specs=pl.BlockSpec((levels // PAIR, step, rows, lat), lambda i: (0, i, 0, 0)),
        scratch_shapes=[pltpu.VMEM((2, lon * levels, lat), jnp.float32)],
        compiler_params=pltpu.CompilerParams(vmem_limit_bytes=56 * 2**20),
        cost_estimate=pl.CostEstimate(flops=members.size, bytes_accessed=4 * members.size, transcendentals=0),
    )(members)


def lat_sums_kernel(x_ref, parts_ref, grads_ref, table_ref, out_ref, packed):
    bands, count, rows, _ = parts_ref.shape
    x = x_ref[0]

    @pl.when(pl.program_id(0) == 0)
    def _():
        for part in range(bands):
            packed[part] = pack_rows(
                [grads_ref[(part + 4 - x) % 4, place].astype(jnp.float32) for place in range(PAIR)], rows
            )

    for m in range(count):
        product = [
            (parts_ref[part, m].astype(jnp.float32) * packed[part]).astype(jnp.bfloat16)
            for part in range(bands)
        ]
        sums = jnp.dot(
            jnp.concatenate(product, axis=1), table_ref[...], preferred_element_type=jnp.float32
        )
        out_ref[m] = sums.astype(jnp.bfloat16)


def lat_sums(x, parts, grads, table):
    bands, count, rows, lat = parts.shape
    waves = table.shape[1]
    step = min(4, count)
    return pl.pallas_call(
        lat_sums_kernel,
        out_shape=pltpu.HBM((count, rows, waves), jnp.bfloat16),
        grid=(count // step,),
        in_specs=[
            pl.BlockSpec(memory_space=pltpu.SMEM),
            pl.BlockSpec((bands, step, rows, lat), lambda i: (0, i, 0, 0)),
            pl.BlockSpec(grads.shape, lambda i: (0, 0, 0, 0)),
            pl.BlockSpec((bands * lat, waves), lambda i: (0, 0)),
        ],
        out_specs=pl.BlockSpec((step, rows, waves), lambda i: (i, 0, 0)),
        scratch_shapes=[pltpu.VMEM((bands, rows, lat), jnp.float32)],
        compiler_params=pltpu.CompilerParams(vmem_limit_bytes=24 * 2**20),
        cost_estimate=pl.CostEstimate(
            flops=2 * parts.size * waves, bytes_accessed=2 * parts.size, transcendentals=0
        ),
    )(jnp.reshape(x, (1,)).astype(jnp.int32), parts, grads, table)


def zonal_kernel(rows_ref, main_ref, tails_ref, out_ref):
    blocks = rows_ref.shape[0]
    whole = main_ref.shape[1] // blocks
    bands = [rows_ref[block].astype(jnp.float32) for block in range(blocks)]
    last = jnp.concatenate([band[PAIR * whole :] for band in bands]).astype(jnp.bfloat16)
    for level in range(PAIR):
        first = [band[level * whole : (level + 1) * whole] for band in bands]
        sums = jnp.dot(
            main_ref[...], jnp.concatenate(first).astype(jnp.bfloat16), preferred_element_type=jnp.float32
        ) + jnp.dot(tails_ref[level], last, preferred_element_type=jnp.float32)
        quarter = sums.shape[0] // 4
        for part in range(4):
            out_ref[part, level] = sums[part * quarter : (part + 1) * quarter].astype(jnp.bfloat16)


def zonal_sums(rows, main, tails):
    waves, k_lat = main.shape[0], rows.shape[2]
    return pl.pallas_call(
        zonal_kernel,
        out_shape=pltpu.HBM((4, PAIR, waves // 4, k_lat), jnp.bfloat16),
        in_specs=[pl.BlockSpec(memory_space=pltpu.VMEM)] * 3,
        out_specs=pl.BlockSpec(memory_space=pltpu.VMEM),
        compiler_params=pltpu.CompilerParams(vmem_limit_bytes=24 * 2**20),
        cost_estimate=pl.CostEstimate(
            flops=2 * PAIR * main.size * k_lat, bytes_accessed=2 * (main.size + rows.size), transcendentals=0
        ),
    )(rows, main, tails)


def local(members, grad_field, static_std, vert_mix, loc_weights):
    mem_local, levels, lon_local, lat_local = members.shape
    mem = lax.axis_index("mem")
    half_z, y = mem // 4, mem % 4
    x = lax.axis_index("lat")
    rows = -(-PAIR * lon_local // TILE) * TILE

    sent = spread(members.transpose(0, 2, 1, 3), rows)
    parts = lax.all_to_all(sent, "lat", split_axis=0, concat_axis=0, tiled=True)

    lat_table = lat_table_make(after(jnp.arange(NLAT, dtype=jnp.int32), sent), NLAT, KLAT)
    own_grad = grad_field[0].astype(jnp.bfloat16)
    far_grad = lax.ppermute(own_grad, "mem", partners(8, 4))
    mine = jnp.stack([jnp.where(half_z == 0, own_grad, far_grad), jnp.where(half_z == 0, far_grad, own_grad)])
    beside = lax.ppermute(mine, "mem", partners(8, 1))
    two = jnp.stack([jnp.where(y % 2 == 0, mine, beside), jnp.where(y % 2 == 0, beside, mine)])
    others = lax.ppermute(two, "mem", partners(8, 3))
    grads = jnp.concatenate([jnp.where(y < 2, two, others), jnp.where(y < 2, others, two)])
    grads = grads.transpose(1, 0, 2, 3).reshape(levels, lon_local, lat_local)
    pairs = grads.reshape(4, PAIR, lon_local, lat_local)

    def pair(step):
        return lax.dynamic_index_in_dim(pairs, (x + step) % 4, 0, keepdims=False)

    met = jnp.stack(
        [pair(0)]
        + [lax.ppermute(pair(4 - d), "lat", [(i, (i - d) % 4) for i in range(4)]) for d in (1, 2, 3)]
    )
    sums = lat_sums(x, parts, met, lat_table)

    whole = lax.all_to_all(sums, "lon", split_axis=0, concat_axis=0, tiled=True)
    waves = after(jnp.arange(KLON, dtype=jnp.int32), sums)
    zonal = zonal_sums(whole, *lon_tables_make(NLON, mem_local, waves))
    alpha = lax.all_to_all(zonal, "lat", split_axis=0, concat_axis=0, tiled=True)
    alpha_grad = alpha.reshape(levels, KLON // 4, KLAT).astype(jnp.float32) * loc_weights[None]

    mix = after(lax.dynamic_index_in_dim(vert_mix, mem, 1, keepdims=False), sums)
    static_grad = jnp.sum(mix[:, None, None] * (static_std * grads.astype(jnp.float32)), axis=0)
    return (alpha_grad, static_grad[None])


def solution(mesh):
    in_specs = (
        P("mem", None, "lon", "lat"),
        P("mem", "lon", "lat"),
        P(None, "lon", "lat"),
        P(),
        P("lat", None),
    )
    out_specs = (P(("mem", "lon"), "lat", None), P("mem", "lon", "lat"))
    return jax.shard_map(local, mesh=mesh, in_specs=in_specs, out_specs=out_specs, check_vma=False)
```

```python
import jax
import jax.numpy as jnp
from jax import lax
from jax.experimental import pallas as pl
from jax.experimental.pallas import tpu as pltpu
from jax.sharding import PartitionSpec as P

NLON = 1440
NLAT = 512
KLON = 512
KLAT = 128
PAIR = 2
TILE = 8


def cosine(phase, period):
    return jnp.cos(jnp.float32(2.0 * jnp.pi) * (phase % period).astype(jnp.float32) / period)


def lon_table_make(n_lon, places, waves):
    half = waves.shape[0] // 2
    sine = waves >= half
    number = jnp.where(sine, waves - half + 1, waves)[:, None]
    phase = number * places[None, :] - jnp.where(sine, n_lon // 4, 0)[:, None]
    return cosine(phase, n_lon) * jnp.sqrt(jnp.float32(2.0) / n_lon)


def lon_tables_make(n_lon, blocks, waves):
    band = n_lon // blocks
    whole = band // TILE * TILE
    left = band - whole
    column = jnp.arange(blocks * whole, dtype=jnp.int32)
    main = lon_table_make(n_lon, column // whole * band + column % whole, waves)
    column = jnp.arange(blocks * TILE, dtype=jnp.int32)
    row = column % TILE
    tail = lon_table_make(n_lon, column // TILE * band + whole + row % left, waves)
    tails = [jnp.where((row // left == level)[None, :], tail, 0.0) for level in range(PAIR)]
    return main.astype(jnp.bfloat16), jnp.stack(tails).astype(jnp.bfloat16)


def lat_table_make(cells, n_lat, k_lat):
    waves = jnp.arange(k_lat, dtype=jnp.int32)[None, :]
    phase = ((2 * cells[:, None] + 1) * waves % (4 * n_lat)).astype(jnp.float32)
    angle = jnp.float32(jnp.pi) * phase / (2 * n_lat)
    return (jnp.cos(angle) * jnp.sqrt(jnp.float32(2.0) / n_lat)).astype(jnp.bfloat16)


def after(value, earlier):
    return lax.optimization_barrier((value, earlier))[0]


def partners(size, flip):
    return [(i, i ^ flip) for i in range(size)]


def to_columns(turn):
    places = [(half, y, x) for half in range(2) for y in range(4) for x in range(4)]
    return [(half * 16 + y * 4 + x, half * 16 + (x + turn) % 4 * 4 + y) for half, y, x in places]


def gather_y(mine, y):
    rings = [[(i, i // 4 * 4 + (i - step) % 4) for i in range(8)] for step in (1, 2, 3)]
    ahead = [lax.ppermute(mine, "mem", pairs) for pairs in rings]
    turned = jnp.stack([mine, *ahead, mine, *ahead[:2]])
    return lax.dynamic_slice_in_dim(turned, (4 - y) % 4, 4, 0)


def pack_rows(fields, rows):
    lon = fields[0].shape[0]
    whole = lon // TILE * TILE
    empty = jnp.zeros((rows - len(fields) * lon, fields[0].shape[1]), fields[0].dtype)
    return jnp.concatenate([*[f[:whole] for f in fields], *[f[whole:] for f in fields], empty])


def spread_kernel(members_ref, out_ref, wide):
    count, lon, levels, lat = members_ref.shape
    whole = lon // TILE * TILE
    rows = out_ref.shape[2]
    for m in range(count):
        wide[m % 2] = members_ref[m].astype(jnp.float32).reshape(lon * levels, lat)
        for part in range(levels // PAIR):
            firsts = [part + place * (levels // PAIR) for place in range(PAIR)]
            pieces = [wide[m % 2, pl.ds(first, whole, stride=levels), :] for first in firsts]
            lasts = [
                wide[m % 2, pl.ds(first + n * levels, 1), :] for first in firsts for n in range(whole, lon)
            ]
            empty = jnp.zeros((rows - PAIR * lon, lat), jnp.float32)
            out_ref[part, m] = jnp.concatenate([*pieces, *lasts, empty]).astype(jnp.bfloat16)


def spread(members, rows):
    count, lon, levels, lat = members.shape
    step = min(4, count)
    return pl.pallas_call(
        spread_kernel,
        out_shape=jax.ShapeDtypeStruct((levels // PAIR, count, rows, lat), members.dtype),
        grid=(count // step,),
        in_specs=[pl.BlockSpec((step, lon, levels, lat), lambda i: (i, 0, 0, 0))],
        out_specs=pl.BlockSpec((levels // PAIR, step, rows, lat), lambda i: (0, i, 0, 0)),
        scratch_shapes=[pltpu.VMEM((2, lon * levels, lat), jnp.float32)],
        compiler_params=pltpu.CompilerParams(vmem_limit_bytes=56 * 2**20),
        cost_estimate=pl.CostEstimate(flops=members.size, bytes_accessed=4 * members.size, transcendentals=0),
    )(members)


def lat_sums_kernel(first_ref, parts_ref, grads_ref, table_ref, out_ref, packed):
    bands, count, rows, _ = parts_ref.shape
    first = first_ref[0]

    @pl.when(pl.program_id(0) == 0)
    def _():
        for part in range(bands):
            packed[part] = pack_rows(
                [grads_ref[(first + 4 - part) % 4, place].astype(jnp.float32) for place in range(PAIR)], rows
            )

    for m in range(count):
        product = [
            (parts_ref[part, m].astype(jnp.float32) * packed[part]).astype(jnp.bfloat16)
            for part in range(bands)
        ]
        sums = jnp.dot(
            jnp.concatenate(product, axis=1), table_ref[...], preferred_element_type=jnp.float32
        )
        out_ref[m] = sums.astype(jnp.bfloat16)


def lat_sums(first, parts, grads, table):
    bands, count, rows, lat = parts.shape
    waves = table.shape[1]
    step = min(4, count)
    return pl.pallas_call(
        lat_sums_kernel,
        out_shape=pltpu.HBM((count, rows, waves), jnp.bfloat16),
        grid=(count // step,),
        in_specs=[
            pl.BlockSpec(memory_space=pltpu.SMEM),
            pl.BlockSpec((bands, step, rows, lat), lambda i: (0, i, 0, 0)),
            pl.BlockSpec(grads.shape, lambda i: (0, 0, 0, 0)),
            pl.BlockSpec((bands * lat, waves), lambda i: (0, 0)),
        ],
        out_specs=pl.BlockSpec((step, rows, waves), lambda i: (i, 0, 0)),
        scratch_shapes=[pltpu.VMEM((bands, rows, lat), jnp.float32)],
        compiler_params=pltpu.CompilerParams(vmem_limit_bytes=24 * 2**20),
        cost_estimate=pl.CostEstimate(
            flops=2 * parts.size * waves, bytes_accessed=2 * parts.size, transcendentals=0
        ),
    )(jnp.reshape(first, (1,)).astype(jnp.int32), parts, grads, table)


def zonal_kernel(rows_ref, main_ref, tails_ref, out_ref):
    blocks = rows_ref.shape[0]
    whole = main_ref.shape[1] // blocks
    bands = [rows_ref[block].astype(jnp.float32) for block in range(blocks)]
    last = jnp.concatenate([band[PAIR * whole :] for band in bands]).astype(jnp.bfloat16)
    for level in range(PAIR):
        first = [band[level * whole : (level + 1) * whole] for band in bands]
        sums = jnp.dot(
            main_ref[...], jnp.concatenate(first).astype(jnp.bfloat16), preferred_element_type=jnp.float32
        ) + jnp.dot(tails_ref[level], last, preferred_element_type=jnp.float32)
        quarter = sums.shape[0] // 4
        for part in range(4):
            out_ref[part, level] = sums[part * quarter : (part + 1) * quarter].astype(jnp.bfloat16)


def zonal_sums(rows, main, tails):
    waves, k_lat = main.shape[0], rows.shape[2]
    return pl.pallas_call(
        zonal_kernel,
        out_shape=pltpu.HBM((4, PAIR, waves // 4, k_lat), jnp.bfloat16),
        in_specs=[pl.BlockSpec(memory_space=pltpu.VMEM)] * 3,
        out_specs=pl.BlockSpec(memory_space=pltpu.VMEM),
        compiler_params=pltpu.CompilerParams(vmem_limit_bytes=24 * 2**20),
        cost_estimate=pl.CostEstimate(
            flops=2 * PAIR * main.size * k_lat, bytes_accessed=2 * (main.size + rows.size), transcendentals=0
        ),
    )(rows, main, tails)


def weighted_kernel(values_ref, weights_ref, out_ref):
    bands = values_ref.shape[0]
    for place in range(PAIR):
        for part in range(bands):
            out_ref[place * bands + part] = values_ref[part, place].astype(jnp.float32) * weights_ref[...]


def weighted(values, weights):
    bands, _, waves, k_lat = values.shape
    return pl.pallas_call(
        weighted_kernel,
        out_shape=jax.ShapeDtypeStruct((bands * PAIR, waves, k_lat), jnp.float32),
        in_specs=[pl.BlockSpec(memory_space=pltpu.VMEM)] * 2,
        out_specs=pl.BlockSpec(memory_space=pltpu.VMEM),
        cost_estimate=pl.CostEstimate(flops=values.size, bytes_accessed=6 * values.size, transcendentals=0),
    )(values, weights)


def local(members, grad_field, static_std, vert_mix, loc_weights):
    mem_local, levels, lon_local, lat_local = members.shape
    mem = lax.axis_index("mem")
    half_z, y = mem // 4, mem % 4
    rows = -(-PAIR * lon_local // TILE) * TILE

    sent = spread(members.transpose(0, 2, 1, 3), rows)
    parts = lax.all_to_all(sent, "lat", split_axis=0, concat_axis=0, tiled=True)

    lat_table = lat_table_make(after(jnp.arange(NLAT, dtype=jnp.int32), sent), NLAT, KLAT)
    own_grad = grad_field[0]
    far_grad = lax.ppermute(own_grad, "mem", partners(8, 4))
    mine = jnp.stack([jnp.where(half_z == 0, own_grad, far_grad), jnp.where(half_z == 0, far_grad, own_grad)])
    met = jnp.stack([lax.ppermute(mine.astype(jnp.bfloat16), ("mem", "lat"), to_columns(j)) for j in range(4)])
    sums = lat_sums(y, parts, met, lat_table)

    whole = lax.all_to_all(sums, "lon", split_axis=0, concat_axis=0, tiled=True)
    waves = after(jnp.arange(KLON, dtype=jnp.int32), sums)
    main, tails = lon_tables_make(NLON, mem_local, waves)
    zonal = zonal_sums(whole, main, tails)
    alpha = lax.all_to_all(zonal, "lat", split_axis=0, concat_axis=0, tiled=True)
    alpha_grad = weighted(alpha, loc_weights)

    grads = gather_y(after(mine, main), y).transpose(1, 0, 2, 3).reshape(levels, lon_local, lat_local)
    mix = after(lax.dynamic_index_in_dim(vert_mix, mem, 1, keepdims=False), sums)
    static_grad = jnp.sum(mix[:, None, None] * (static_std * grads), axis=0)
    return (alpha_grad, static_grad[None])


def solution(mesh):
    in_specs = (
        P("mem", None, "lon", "lat"),
        P("mem", "lon", "lat"),
        P(None, "lon", "lat"),
        P(),
        P("lat", None),
    )
    out_specs = (P(("mem", "lon"), "lat", None), P("mem", "lon", "lat"))
    return jax.shard_map(local, mesh=mesh, in_specs=in_specs, out_specs=out_specs, check_vma=False)
```

```python
import jax
import jax.numpy as jnp
from jax import lax
from jax.experimental import pallas as pl
from jax.experimental.pallas import tpu as pltpu
from jax.sharding import PartitionSpec as P

NLON = 1440
NLAT = 512
KLON = 512
KLAT = 128
PAIR = 2
TILE = 8


def cosine(phase, period):
    return jnp.cos(jnp.float32(2.0 * jnp.pi) * (phase % period).astype(jnp.float32) / period)


def lon_table_make(n_lon, places, waves):
    half = waves.shape[0] // 2
    sine = waves >= half
    number = jnp.where(sine, waves - half + 1, waves)[:, None]
    phase = number * places[None, :] - jnp.where(sine, n_lon // 4, 0)[:, None]
    return cosine(phase, n_lon) * jnp.sqrt(jnp.float32(2.0) / n_lon)


def lon_tables_make(n_lon, blocks, waves):
    band = n_lon // blocks
    whole = band // TILE * TILE
    left = band - whole
    column = jnp.arange(blocks * whole, dtype=jnp.int32)
    main = lon_table_make(n_lon, column // whole * band + column % whole, waves)
    column = jnp.arange(blocks * TILE, dtype=jnp.int32)
    row = column % TILE
    tail = lon_table_make(n_lon, column // TILE * band + whole + row % left, waves)
    tails = [jnp.where((row // left == level)[None, :], tail, 0.0) for level in range(PAIR)]
    return main.astype(jnp.bfloat16), jnp.stack(tails).astype(jnp.bfloat16)


def lat_table_make(cells, n_lat, k_lat):
    waves = jnp.arange(k_lat, dtype=jnp.int32)[None, :]
    phase = ((2 * cells[:, None] + 1) * waves % (4 * n_lat)).astype(jnp.float32)
    angle = jnp.float32(jnp.pi) * phase / (2 * n_lat)
    return (jnp.cos(angle) * jnp.sqrt(jnp.float32(2.0) / n_lat)).astype(jnp.bfloat16)


def after(value, earlier):
    return lax.optimization_barrier((value, earlier))[0]


def partners(size, flip):
    return [(i, i ^ flip) for i in range(size)]


def pack_rows(fields, rows):
    lon = fields[0].shape[0]
    whole = lon // TILE * TILE
    empty = jnp.zeros((rows - len(fields) * lon, fields[0].shape[1]), fields[0].dtype)
    return jnp.concatenate([*[f[:whole] for f in fields], *[f[whole:] for f in fields], empty])


def spread_kernel(members_ref, out_ref, wide):
    count, lon, levels, lat = members_ref.shape
    whole = lon // TILE * TILE
    rows = out_ref.shape[2]
    for m in range(count):
        wide[m % 2] = members_ref[m].astype(jnp.float32).reshape(lon * levels, lat)
        for part in range(levels // PAIR):
            firsts = [part * PAIR + place for place in range(PAIR)]
            pieces = [wide[m % 2, pl.ds(first, whole, stride=levels), :] for first in firsts]
            lasts = [
                wide[m % 2, pl.ds(first + n * levels, 1), :] for first in firsts for n in range(whole, lon)
            ]
            empty = jnp.zeros((rows - PAIR * lon, lat), jnp.float32)
            out_ref[part, m] = jnp.concatenate([*pieces, *lasts, empty]).astype(jnp.bfloat16)


def spread(members, rows):
    count, lon, levels, lat = members.shape
    step = min(4, count)
    return pl.pallas_call(
        spread_kernel,
        out_shape=jax.ShapeDtypeStruct((levels // PAIR, count, rows, lat), members.dtype),
        grid=(count // step,),
        in_specs=[pl.BlockSpec((step, lon, levels, lat), lambda i: (i, 0, 0, 0))],
        out_specs=pl.BlockSpec((levels // PAIR, step, rows, lat), lambda i: (0, i, 0, 0)),
        scratch_shapes=[pltpu.VMEM((2, lon * levels, lat), jnp.float32)],
        compiler_params=pltpu.CompilerParams(vmem_limit_bytes=56 * 2**20),
        cost_estimate=pl.CostEstimate(flops=members.size, bytes_accessed=4 * members.size, transcendentals=0),
    )(members)


def lat_sums_kernel(x_ref, parts_ref, grads_ref, table_ref, out_ref, packed, sums, done):
    bands, count, rows, _ = parts_ref.shape
    x = x_ref[0]
    group = count // done.shape[0]

    def to_out(i):
        span = pl.ds(i * group, group)
        return pltpu.make_async_copy(sums.at[span], out_ref.at[span], done.at[i])

    for part in range(bands):
        packed[part] = pack_rows([grads_ref[(part + 4 - x) % 4, place] for place in range(PAIR)], rows)
    for m in range(count):
        product = [
            (parts_ref[part, m].astype(jnp.float32) * packed[part]).astype(jnp.bfloat16)
            for part in range(bands)
        ]
        sums[m] = jnp.dot(
            jnp.concatenate(product, axis=1), table_ref[...], preferred_element_type=jnp.float32
        ).astype(jnp.bfloat16)
        if m % group == group - 1:
            to_out(m // group).start()
    for i in range(done.shape[0]):
        to_out(i).wait()


def lat_sums(x, parts, grads, table):
    bands, count, rows, lat = parts.shape
    waves = table.shape[1]
    return pl.pallas_call(
        lat_sums_kernel,
        out_shape=pltpu.HBM((count, rows, waves), jnp.bfloat16),
        in_specs=[pl.BlockSpec(memory_space=pltpu.SMEM)] + [pl.BlockSpec(memory_space=pltpu.VMEM)] * 3,
        out_specs=pl.BlockSpec(memory_space=pltpu.HBM),
        scratch_shapes=[
            pltpu.VMEM((bands, rows, lat), jnp.float32),
            pltpu.VMEM((count, rows, waves), jnp.bfloat16),
            pltpu.SemaphoreType.DMA((min(4, count),)),
        ],
        compiler_params=pltpu.CompilerParams(vmem_limit_bytes=24 * 2**20),
        cost_estimate=pl.CostEstimate(
            flops=2 * parts.size * waves, bytes_accessed=2 * parts.size, transcendentals=0
        ),
    )(jnp.reshape(x, (1,)).astype(jnp.int32), parts, grads, table)


def zonal_kernel(rows_ref, main_ref, tails_ref, out_ref):
    blocks = rows_ref.shape[0]
    whole = main_ref.shape[1] // blocks
    bands = [rows_ref[block].astype(jnp.float32) for block in range(blocks)]
    last = jnp.concatenate([band[PAIR * whole :] for band in bands]).astype(jnp.bfloat16)
    for level in range(PAIR):
        first = [band[level * whole : (level + 1) * whole] for band in bands]
        sums = jnp.dot(
            main_ref[...], jnp.concatenate(first).astype(jnp.bfloat16), preferred_element_type=jnp.float32
        ) + jnp.dot(tails_ref[level], last, preferred_element_type=jnp.float32)
        quarter = sums.shape[0] // 4
        for part in range(4):
            out_ref[part, level] = sums[part * quarter : (part + 1) * quarter].astype(jnp.bfloat16)


def zonal_sums(rows, main, tails):
    waves, k_lat = main.shape[0], rows.shape[2]
    return pl.pallas_call(
        zonal_kernel,
        out_shape=pltpu.HBM((4, PAIR, waves // 4, k_lat), jnp.bfloat16),
        in_specs=[pl.BlockSpec(memory_space=pltpu.VMEM)] * 3,
        out_specs=pl.BlockSpec(memory_space=pltpu.VMEM),
        compiler_params=pltpu.CompilerParams(vmem_limit_bytes=24 * 2**20),
        cost_estimate=pl.CostEstimate(
            flops=2 * PAIR * main.size * k_lat, bytes_accessed=2 * (main.size + rows.size), transcendentals=0
        ),
    )(rows, main, tails)


def local(members, grad_field, static_std, vert_mix, loc_weights):
    mem_local, levels, lon_local, lat_local = members.shape
    mem = lax.axis_index("mem")
    half_z, y = mem // 4, mem % 4
    x = lax.axis_index("lat")
    rows = -(-PAIR * lon_local // TILE) * TILE

    sent = spread(members.transpose(0, 2, 1, 3), rows)
    parts = lax.all_to_all(sent, "lat", split_axis=0, concat_axis=0, tiled=True)

    lat_table = lat_table_make(after(jnp.arange(NLAT, dtype=jnp.int32), sent), NLAT, KLAT)
    own_grad = grad_field[0]
    far_grad = lax.ppermute(own_grad, "mem", partners(8, 4))
    mine = jnp.stack([jnp.where(half_z == 0, own_grad, far_grad), jnp.where(half_z == 0, far_grad, own_grad)])
    beside = lax.ppermute(mine, "mem", partners(8, 1))
    two = jnp.stack([jnp.where(y % 2 == 0, mine, beside), jnp.where(y % 2 == 0, beside, mine)])
    others = lax.ppermute(two, "mem", partners(8, 3))
    grads = jnp.concatenate([jnp.where(y < 2, two, others), jnp.where(y < 2, others, two)])
    grads = grads.transpose(1, 0, 2, 3).reshape(levels, lon_local, lat_local)
    pairs = grads.reshape(4, PAIR, lon_local, lat_local)

    def pair(step):
        return lax.dynamic_index_in_dim(pairs, (x + step) % 4, 0, keepdims=False)

    met = jnp.stack(
        [pair(0)]
        + [lax.ppermute(pair(4 - d), "lat", [(i, (i - d) % 4) for i in range(4)]) for d in (1, 2, 3)]
    )
    sums = lat_sums(x, parts, met, lat_table)

    whole = lax.all_to_all(sums, "lon", split_axis=0, concat_axis=0, tiled=True)
    waves = after(jnp.arange(KLON, dtype=jnp.int32), sums)
    zonal = zonal_sums(whole, *lon_tables_make(NLON, mem_local, waves))
    alpha = lax.all_to_all(zonal, "lat", split_axis=0, concat_axis=0, tiled=True)
    alpha_grad = alpha.reshape(levels, KLON // 4, KLAT).astype(jnp.float32) * loc_weights[None]

    mix = after(lax.dynamic_index_in_dim(vert_mix, mem, 1, keepdims=False), sums)
    static_grad = jnp.sum(mix[:, None, None] * (static_std * grads), axis=0)
    return (alpha_grad, static_grad[None])


def solution(mesh):
    in_specs = (
        P("mem", None, "lon", "lat"),
        P("mem", "lon", "lat"),
        P(None, "lon", "lat"),
        P(),
        P("lat", None),
    )
    out_specs = (P(("mem", "lon"), "lat", None), P("mem", "lon", "lat"))
    return jax.shard_map(local, mesh=mesh, in_specs=in_specs, out_specs=out_specs, check_vma=False)
```

```python
import jax
import jax.numpy as jnp
from jax import lax
from jax.experimental import pallas as pl
from jax.experimental.pallas import tpu as pltpu
from jax.sharding import PartitionSpec as P

NLON = 1440
NLAT = 512
KLON = 512
KLAT = 128
PAIR = 2
TILE = 8


def cosine(phase, period):
    return jnp.cos(jnp.float32(2.0 * jnp.pi) * (phase % period).astype(jnp.float32) / period)


def lon_table_make(n_lon, places, waves):
    half = waves.shape[0] // 2
    sine = waves >= half
    number = jnp.where(sine, waves - half + 1, waves)[:, None]
    phase = number * places[None, :] - jnp.where(sine, n_lon // 4, 0)[:, None]
    return cosine(phase, n_lon) * jnp.sqrt(jnp.float32(2.0) / n_lon)


def lon_tables_make(n_lon, blocks, waves):
    band = n_lon // blocks
    whole = band // TILE * TILE
    left = band - whole
    column = jnp.arange(blocks * whole, dtype=jnp.int32)
    main = lon_table_make(n_lon, column // whole * band + column % whole, waves)
    column = jnp.arange(blocks * TILE, dtype=jnp.int32)
    row = column % TILE
    tail = lon_table_make(n_lon, column // TILE * band + whole + row % left, waves)
    tails = [jnp.where((row // left == level)[None, :], tail, 0.0) for level in range(PAIR)]
    return main.astype(jnp.bfloat16), jnp.stack(tails).astype(jnp.bfloat16)


def lat_table_make(cells, n_lat, k_lat):
    waves = jnp.arange(k_lat, dtype=jnp.int32)[None, :]
    phase = ((2 * cells[:, None] + 1) * waves % (4 * n_lat)).astype(jnp.float32)
    angle = jnp.float32(jnp.pi) * phase / (2 * n_lat)
    return (jnp.cos(angle) * jnp.sqrt(jnp.float32(2.0) / n_lat)).astype(jnp.bfloat16)


def after(value, earlier):
    return lax.optimization_barrier((value, earlier))[0]


def partners(size, flip):
    return [(i, i ^ flip) for i in range(size)]


def pack_rows(fields, rows):
    lon = fields[0].shape[0]
    whole = lon // TILE * TILE
    empty = jnp.zeros((rows - len(fields) * lon, fields[0].shape[1]), fields[0].dtype)
    return jnp.concatenate([*[f[:whole] for f in fields], *[f[whole:] for f in fields], empty])


def spread_kernel(members_ref, out_ref, held, wide, spread_out, arrived, done):
    count, lon, levels, lat = held.shape
    whole = lon // TILE * TILE
    rows = out_ref.shape[2]
    group = count // done.shape[0]

    def to_held(m):
        return pltpu.make_async_copy(members_ref.at[m], held.at[m], arrived.at[m])

    def to_out(i):
        span = pl.ds(i * group, group)
        return pltpu.make_async_copy(spread_out.at[:, span], out_ref.at[:, span], done.at[i])

    for m in range(count):
        to_held(m).start()
    for m in range(count):
        to_held(m).wait()
        wide[m % 2] = held[m].astype(jnp.float32).reshape(lon * levels, lat)
        for part in range(levels // PAIR):
            firsts = [part * PAIR + place for place in range(PAIR)]
            pieces = [wide[m % 2, pl.ds(first, whole, stride=levels), :] for first in firsts]
            lasts = [
                wide[m % 2, pl.ds(first + n * levels, 1), :] for first in firsts for n in range(whole, lon)
            ]
            empty = jnp.zeros((rows - PAIR * lon, lat), jnp.float32)
            spread_out[part, m] = jnp.concatenate([*pieces, *lasts, empty]).astype(jnp.bfloat16)
        if m % group == group - 1:
            to_out(m // group).start()
    for i in range(done.shape[0]):
        to_out(i).wait()


def spread(members, rows):
    count, lon, levels, lat = members.shape
    shape = (levels // PAIR, count, rows, lat)
    return pl.pallas_call(
        spread_kernel,
        out_shape=pltpu.HBM(shape, members.dtype),
        in_specs=[pl.BlockSpec(memory_space=pltpu.HBM)],
        out_specs=pl.BlockSpec(memory_space=pltpu.HBM),
        scratch_shapes=[
            pltpu.VMEM(members.shape, members.dtype),
            pltpu.VMEM((2, lon * levels, lat), jnp.float32),
            pltpu.VMEM(shape, members.dtype),
            pltpu.SemaphoreType.DMA((count,)),
            pltpu.SemaphoreType.DMA((max(1, count // 2),)),
        ],
        compiler_params=pltpu.CompilerParams(vmem_limit_bytes=56 * 2**20),
        cost_estimate=pl.CostEstimate(flops=members.size, bytes_accessed=4 * members.size, transcendentals=0),
    )(members)


def lat_sums_kernel(x_ref, parts_ref, grads_ref, table_ref, out_ref, packed, sums, done):
    bands, count, rows, _ = parts_ref.shape
    x = x_ref[0]
    group = count // done.shape[0]

    def to_out(i):
        span = pl.ds(i * group, group)
        return pltpu.make_async_copy(sums.at[span], out_ref.at[span], done.at[i])

    for part in range(bands):
        packed[part] = pack_rows([grads_ref[(part + 4 - x) % 4, place] for place in range(PAIR)], rows)
    for m in range(count):
        product = [
            (parts_ref[part, m].astype(jnp.float32) * packed[part]).astype(jnp.bfloat16)
            for part in range(bands)
        ]
        sums[m] = jnp.dot(
            jnp.concatenate(product, axis=1), table_ref[...], preferred_element_type=jnp.float32
        ).astype(jnp.bfloat16)
        if m % group == group - 1:
            to_out(m // group).start()
    for i in range(done.shape[0]):
        to_out(i).wait()


def lat_sums(x, parts, grads, table):
    bands, count, rows, lat = parts.shape
    waves = table.shape[1]
    return pl.pallas_call(
        lat_sums_kernel,
        out_shape=pltpu.HBM((count, rows, waves), jnp.bfloat16),
        in_specs=[pl.BlockSpec(memory_space=pltpu.SMEM)] + [pl.BlockSpec(memory_space=pltpu.VMEM)] * 3,
        out_specs=pl.BlockSpec(memory_space=pltpu.HBM),
        scratch_shapes=[
            pltpu.VMEM((bands, rows, lat), jnp.float32),
            pltpu.VMEM((count, rows, waves), jnp.bfloat16),
            pltpu.SemaphoreType.DMA((min(4, count),)),
        ],
        compiler_params=pltpu.CompilerParams(vmem_limit_bytes=24 * 2**20),
        cost_estimate=pl.CostEstimate(
            flops=2 * parts.size * waves, bytes_accessed=2 * parts.size, transcendentals=0
        ),
    )(jnp.reshape(x, (1,)).astype(jnp.int32), parts, grads, table)


def zonal_kernel(rows_ref, main_ref, tails_ref, out_ref):
    blocks = rows_ref.shape[0]
    whole = main_ref.shape[1] // blocks
    bands = [rows_ref[block].astype(jnp.float32) for block in range(blocks)]
    last = jnp.concatenate([band[PAIR * whole :] for band in bands]).astype(jnp.bfloat16)
    for level in range(PAIR):
        first = [band[level * whole : (level + 1) * whole] for band in bands]
        sums = jnp.dot(
            main_ref[...], jnp.concatenate(first).astype(jnp.bfloat16), preferred_element_type=jnp.float32
        ) + jnp.dot(tails_ref[level], last, preferred_element_type=jnp.float32)
        quarter = sums.shape[0] // 4
        for part in range(4):
            out_ref[part, level] = sums[part * quarter : (part + 1) * quarter].astype(jnp.bfloat16)


def zonal_sums(rows, main, tails):
    waves, k_lat = main.shape[0], rows.shape[2]
    return pl.pallas_call(
        zonal_kernel,
        out_shape=pltpu.HBM((4, PAIR, waves // 4, k_lat), jnp.bfloat16),
        in_specs=[pl.BlockSpec(memory_space=pltpu.VMEM)] * 3,
        out_specs=pl.BlockSpec(memory_space=pltpu.VMEM),
        compiler_params=pltpu.CompilerParams(vmem_limit_bytes=24 * 2**20),
        cost_estimate=pl.CostEstimate(
            flops=2 * PAIR * main.size * k_lat, bytes_accessed=2 * (main.size + rows.size), transcendentals=0
        ),
    )(rows, main, tails)


def local(members, grad_field, static_std, vert_mix, loc_weights):
    mem_local, levels, lon_local, lat_local = members.shape
    mem = lax.axis_index("mem")
    half_z, y = mem // 4, mem % 4
    x = lax.axis_index("lat")
    rows = -(-PAIR * lon_local // TILE) * TILE

    sent = spread(members.transpose(0, 2, 1, 3), rows)
    parts = lax.all_to_all(sent, "lat", split_axis=0, concat_axis=0, tiled=True)

    lat_table = lat_table_make(after(jnp.arange(NLAT, dtype=jnp.int32), sent), NLAT, KLAT)
    own_grad = grad_field[0]
    far_grad = lax.ppermute(own_grad, "mem", partners(8, 4))
    mine = jnp.stack([jnp.where(half_z == 0, own_grad, far_grad), jnp.where(half_z == 0, far_grad, own_grad)])
    beside = lax.ppermute(mine, "mem", partners(8, 1))
    two = jnp.stack([jnp.where(y % 2 == 0, mine, beside), jnp.where(y % 2 == 0, beside, mine)])
    others = lax.ppermute(two, "mem", partners(8, 3))
    grads = jnp.concatenate([jnp.where(y < 2, two, others), jnp.where(y < 2, others, two)])
    grads = grads.transpose(1, 0, 2, 3).reshape(levels, lon_local, lat_local)
    pairs = grads.reshape(4, PAIR, lon_local, lat_local)

    def pair(step):
        return lax.dynamic_index_in_dim(pairs, (x + step) % 4, 0, keepdims=False)

    met = jnp.stack(
        [pair(0)]
        + [lax.ppermute(pair(4 - d), "lat", [(i, (i - d) % 4) for i in range(4)]) for d in (1, 2, 3)]
    )
    sums = lat_sums(x, parts, met, lat_table)

    whole = lax.all_to_all(sums, "lon", split_axis=0, concat_axis=0, tiled=True)
    waves = after(jnp.arange(KLON, dtype=jnp.int32), sums)
    zonal = zonal_sums(whole, *lon_tables_make(NLON, mem_local, waves))
    alpha = lax.all_to_all(zonal, "lat", split_axis=0, concat_axis=0, tiled=True)
    alpha_grad = alpha.reshape(levels, KLON // 4, KLAT).astype(jnp.float32) * loc_weights[None]

    mix = after(lax.dynamic_index_in_dim(vert_mix, mem, 1, keepdims=False), sums)
    static_grad = jnp.sum(mix[:, None, None] * (static_std * grads), axis=0)
    return (alpha_grad, static_grad[None])


def solution(mesh):
    in_specs = (
        P("mem", None, "lon", "lat"),
        P("mem", "lon", "lat"),
        P(None, "lon", "lat"),
        P(),
        P("lat", None),
    )
    out_specs = (P(("mem", "lon"), "lat", None), P("mem", "lon", "lat"))
    return jax.shard_map(local, mesh=mesh, in_specs=in_specs, out_specs=out_specs, check_vma=False)
```

```python
import jax
import jax.numpy as jnp
from jax import lax
from jax.experimental import pallas as pl
from jax.experimental.pallas import tpu as pltpu
from jax.sharding import PartitionSpec as P

NLON = 1440
NLAT = 512
KLON = 512
KLAT = 128
PAIR = 2
TILE = 8


def cosine(phase, period):
    return jnp.cos(jnp.float32(2.0 * jnp.pi) * (phase % period).astype(jnp.float32) / period)


def lon_table_make(n_lon, places, waves):
    half = waves.shape[0] // 2
    sine = waves >= half
    number = jnp.where(sine, waves - half + 1, waves)[:, None]
    phase = number * places[None, :] - jnp.where(sine, n_lon // 4, 0)[:, None]
    return cosine(phase, n_lon) * jnp.sqrt(jnp.float32(2.0) / n_lon)


def lon_tables_make(n_lon, blocks, waves):
    band = n_lon // blocks
    whole = band // TILE * TILE
    left = band - whole
    column = jnp.arange(blocks * whole, dtype=jnp.int32)
    main = lon_table_make(n_lon, column // whole * band + column % whole, waves)
    column = jnp.arange(blocks * TILE, dtype=jnp.int32)
    row = column % TILE
    tail = lon_table_make(n_lon, column // TILE * band + whole + row % left, waves)
    tails = [jnp.where((row // left == level)[None, :], tail, 0.0) for level in range(PAIR)]
    return main.astype(jnp.bfloat16), jnp.stack(tails).astype(jnp.bfloat16)


def lat_table_make(cells, n_lat, k_lat):
    waves = jnp.arange(k_lat, dtype=jnp.int32)[None, :]
    phase = ((2 * cells[:, None] + 1) * waves % (4 * n_lat)).astype(jnp.float32)
    angle = jnp.float32(jnp.pi) * phase / (2 * n_lat)
    return (jnp.cos(angle) * jnp.sqrt(jnp.float32(2.0) / n_lat)).astype(jnp.bfloat16)


def after(value, earlier):
    return lax.optimization_barrier((value, earlier))[0]


def partners(size, flip):
    return [(i, i ^ flip) for i in range(size)]


def pack_rows(fields, rows):
    lon = fields[0].shape[0]
    whole = lon // TILE * TILE
    empty = jnp.zeros((rows - len(fields) * lon, fields[0].shape[1]), fields[0].dtype)
    return jnp.concatenate([*[f[:whole] for f in fields], *[f[whole:] for f in fields], empty])


def spread_kernel(members_ref, out_ref, held, wide, spread_out, arrived, done):
    count, lon, levels, lat = held.shape
    whole = lon // TILE * TILE
    rows = out_ref.shape[2]
    group = count // done.shape[0]

    def to_held(m):
        return pltpu.make_async_copy(members_ref.at[m], held.at[m], arrived.at[m])

    def to_out(i):
        span = pl.ds(i * group, group)
        return pltpu.make_async_copy(spread_out.at[:, span], out_ref.at[:, span], done.at[i])

    for m in range(count):
        to_held(m).start()
    for m in range(count):
        to_held(m).wait()
        wide[m % 2, : lon * levels] = held[m].astype(jnp.float32).reshape(lon * levels, lat)
        for part in range(levels // PAIR):
            firsts = [part * PAIR + place for place in range(PAIR)]
            pieces = [wide[m % 2, pl.ds(first, whole, stride=levels), :] for first in firsts]
            lasts = [
                wide[m % 2, pl.ds(first + whole * levels, lon - whole, stride=levels), :] for first in firsts
            ]
            empty = jnp.zeros((rows - PAIR * lon, lat), jnp.float32)
            spread_out[part, m] = jnp.concatenate([*pieces, *lasts, empty]).astype(jnp.bfloat16)
        if m % group == group - 1:
            to_out(m // group).start()
    for i in range(done.shape[0]):
        to_out(i).wait()


def spread(members, rows):
    count, lon, levels, lat = members.shape
    shape = (levels // PAIR, count, rows, lat)
    return pl.pallas_call(
        spread_kernel,
        out_shape=pltpu.HBM(shape, members.dtype),
        in_specs=[pl.BlockSpec(memory_space=pltpu.HBM)],
        out_specs=pl.BlockSpec(memory_space=pltpu.HBM),
        scratch_shapes=[
            pltpu.VMEM(members.shape, members.dtype),
            pltpu.VMEM((2, (lon + TILE) * levels, lat), jnp.float32),
            pltpu.VMEM(shape, members.dtype),
            pltpu.SemaphoreType.DMA((count,)),
            pltpu.SemaphoreType.DMA((max(1, count // 2),)),
        ],
        compiler_params=pltpu.CompilerParams(vmem_limit_bytes=56 * 2**20),
        cost_estimate=pl.CostEstimate(flops=members.size, bytes_accessed=4 * members.size, transcendentals=0),
    )(members)


def lat_sums_kernel(x_ref, parts_ref, grads_ref, table_ref, out_ref, packed, sums, done):
    bands, count, rows, _ = parts_ref.shape
    x = x_ref[0]
    group = count // done.shape[0]

    def to_out(i):
        span = pl.ds(i * group, group)
        return pltpu.make_async_copy(sums.at[span], out_ref.at[span], done.at[i])

    for part in range(bands):
        packed[part] = pack_rows([grads_ref[(part + 4 - x) % 4, place] for place in range(PAIR)], rows)
    for m in range(count):
        product = [
            (parts_ref[part, m].astype(jnp.float32) * packed[part]).astype(jnp.bfloat16)
            for part in range(bands)
        ]
        sums[m] = jnp.dot(
            jnp.concatenate(product, axis=1), table_ref[...], preferred_element_type=jnp.float32
        ).astype(jnp.bfloat16)
        if m % group == group - 1:
            to_out(m // group).start()
    for i in range(done.shape[0]):
        to_out(i).wait()


def lat_sums(x, parts, grads, table):
    bands, count, rows, lat = parts.shape
    waves = table.shape[1]
    return pl.pallas_call(
        lat_sums_kernel,
        out_shape=pltpu.HBM((count, rows, waves), jnp.bfloat16),
        in_specs=[pl.BlockSpec(memory_space=pltpu.SMEM)] + [pl.BlockSpec(memory_space=pltpu.VMEM)] * 3,
        out_specs=pl.BlockSpec(memory_space=pltpu.HBM),
        scratch_shapes=[
            pltpu.VMEM((bands, rows, lat), jnp.float32),
            pltpu.VMEM((count, rows, waves), jnp.bfloat16),
            pltpu.SemaphoreType.DMA((min(4, count),)),
        ],
        compiler_params=pltpu.CompilerParams(vmem_limit_bytes=24 * 2**20),
        cost_estimate=pl.CostEstimate(
            flops=2 * parts.size * waves, bytes_accessed=2 * parts.size, transcendentals=0
        ),
    )(jnp.reshape(x, (1,)).astype(jnp.int32), parts, grads, table)


def zonal_kernel(rows_ref, main_ref, tails_ref, out_ref, sums_ref, done):
    blocks = rows_ref.shape[0]
    whole = main_ref.shape[1] // blocks
    bands = [rows_ref[block].astype(jnp.float32) for block in range(blocks)]

    def to_out(level):
        return pltpu.make_async_copy(sums_ref.at[:, level], out_ref.at[:, level], done.at[level])

    last = jnp.concatenate([band[PAIR * whole :] for band in bands]).astype(jnp.bfloat16)
    for level in range(PAIR):
        first = [band[level * whole : (level + 1) * whole] for band in bands]
        sums = jnp.dot(
            main_ref[...], jnp.concatenate(first).astype(jnp.bfloat16), preferred_element_type=jnp.float32
        ) + jnp.dot(tails_ref[level], last, preferred_element_type=jnp.float32)
        quarter = sums.shape[0] // 4
        for part in range(4):
            sums_ref[part, level] = sums[part * quarter : (part + 1) * quarter].astype(jnp.bfloat16)
        to_out(level).start()
    for level in range(PAIR):
        to_out(level).wait()


def zonal_sums(rows, main, tails):
    waves, k_lat = main.shape[0], rows.shape[2]
    return pl.pallas_call(
        zonal_kernel,
        out_shape=pltpu.HBM((4, PAIR, waves // 4, k_lat), jnp.bfloat16),
        in_specs=[pl.BlockSpec(memory_space=pltpu.VMEM)] * 3,
        out_specs=pl.BlockSpec(memory_space=pltpu.HBM),
        scratch_shapes=[
            pltpu.VMEM((4, PAIR, waves // 4, k_lat), jnp.bfloat16),
            pltpu.SemaphoreType.DMA((PAIR,)),
        ],
        compiler_params=pltpu.CompilerParams(vmem_limit_bytes=24 * 2**20),
        cost_estimate=pl.CostEstimate(
            flops=2 * PAIR * main.size * k_lat, bytes_accessed=2 * (main.size + rows.size), transcendentals=0
        ),
    )(rows, main, tails)


def local(members, grad_field, static_std, vert_mix, loc_weights):
    mem_local, levels, lon_local, lat_local = members.shape
    mem = lax.axis_index("mem")
    half_z, y = mem // 4, mem % 4
    x = lax.axis_index("lat")
    rows = -(-PAIR * lon_local // TILE) * TILE

    sent = spread(members.transpose(0, 2, 1, 3), rows)
    parts = lax.all_to_all(sent, "lat", split_axis=0, concat_axis=0, tiled=True)

    lat_table = lat_table_make(after(jnp.arange(NLAT, dtype=jnp.int32), sent), NLAT, KLAT)
    own_grad = grad_field[0]
    far_grad = lax.ppermute(own_grad, "mem", partners(8, 4))
    mine = jnp.stack([jnp.where(half_z == 0, own_grad, far_grad), jnp.where(half_z == 0, far_grad, own_grad)])
    beside = lax.ppermute(mine, "mem", partners(8, 1))
    two = jnp.stack([jnp.where(y % 2 == 0, mine, beside), jnp.where(y % 2 == 0, beside, mine)])
    others = lax.ppermute(two, "mem", partners(8, 3))
    grads = jnp.concatenate([jnp.where(y < 2, two, others), jnp.where(y < 2, others, two)])
    grads = grads.transpose(1, 0, 2, 3).reshape(levels, lon_local, lat_local)
    pairs = grads.reshape(4, PAIR, lon_local, lat_local)

    def pair(step):
        return lax.dynamic_index_in_dim(pairs, (x + step) % 4, 0, keepdims=False)

    met = jnp.stack(
        [pair(0)]
        + [lax.ppermute(pair(4 - d), "lat", [(i, (i - d) % 4) for i in range(4)]) for d in (1, 2, 3)]
    )
    sums = lat_sums(x, parts, met, lat_table)

    whole = lax.all_to_all(sums, "lon", split_axis=0, concat_axis=0, tiled=True)
    waves = after(jnp.arange(KLON, dtype=jnp.int32), sums)
    zonal = zonal_sums(whole, *lon_tables_make(NLON, mem_local, waves))
    alpha = lax.all_to_all(zonal, "lat", split_axis=0, concat_axis=0, tiled=True)
    alpha_grad = alpha.reshape(levels, KLON // 4, KLAT).astype(jnp.float32) * loc_weights[None]

    mix = after(lax.dynamic_index_in_dim(vert_mix, mem, 1, keepdims=False), sums)
    static_grad = jnp.sum(mix[:, None, None] * (static_std * grads), axis=0)
    return (alpha_grad, static_grad[None])


def solution(mesh):
    in_specs = (
        P("mem", None, "lon", "lat"),
        P("mem", "lon", "lat"),
        P(None, "lon", "lat"),
        P(),
        P("lat", None),
    )
    out_specs = (P(("mem", "lon"), "lat", None), P("mem", "lon", "lat"))
    return jax.shard_map(local, mesh=mesh, in_specs=in_specs, out_specs=out_specs, check_vma=False)
```
